32 devices in a mesh: groups: 2 (over y), pool: 8 (over z, x), tp: 2 (over core).
Axes of the slice: x: 2, y: 2, z: 4, core: 2. Of those that a mesh axis runs over, the one named last changes fastest.
Arguments:
- hidden_rows: bfloat16 [2048, 8192], P(('groups', 'pool'), 'tp'), parts along dimension 0, may hold values from -6 to 6
- base_out: bfloat16 [2048, 8192], P(('groups', 'pool'), 'tp'), parts along dimension 0, may hold values from -6 to 6
- row_adapter: int32 [2048, 1], P(('groups', 'pool')), parts along dimension 0, may hold values from 0 to 7; in each aligned block of 128 rows (0 to 127, 128 to 255, ...) at most 32 rows name the same one
- adapter_slot: int32 [8], replicated, may hold values from 0 to 7, each once
- shrink_pool: bfloat16 [8, 8192, 64], P('pool', 'tp'), may hold values from -0.0625 to 0.0625
- expand_pool: bfloat16 [8, 64, 8192], P('pool', None, 'tp'), may hold values from -0.75 to 0.75
Outputs:
- query_out: bfloat16 [2048, 8192], P(('groups', 'pool'), 'tp'), parts along dimension 0
The draws below stay inside these ranges and needn't reach their ends.
There are 2 independent parts, one for each index of `groups`. The reference program is written for one: setup_inputs(seed, part) draws one part's arguments, and reference() takes and returns one part's arrays. A program takes and returns all parts, laid end to end along the dimension named above; an argument that names none is the same for every part. Nothing has to cross between parts.
Inputs may be any that keep to these rules, and one draw needn't show every extreme that they name: `row_adapter`: among the rows of one pool index, no adapter id stands on more than 32 rows, and some adapter stands on exactly 32 rows in some of them. `adapter_slot`: each adapter has one slot; each slot holds one adapter.
All inputs are finite; a program needn't handle non-finite values.
Results may differ from the reference program's by a relative error of at most 0.0055.
Values may be sent and summed in bfloat16 or wider, within the bound.
A program may use at most 64 MiB of HBM per device.

```python
import math
import jax
import jax.numpy as jnp
import numpy as np
from jax import lax

D = 8192
OUT = 8192
R = 64
ROWS_DEV = 128
ROWS = 1024
ADAPTERS = 8
C = 32


def level_of(own_key, dims, pieces, low, high):
    def one(dim, parts):
        steps = jax.random.uniform(jax.random.fold_in(jax.random.fold_in(own_key, 6), dim), (parts,), jnp.float32, low / len(pieces), high / len(pieces))
        return jnp.repeat(jnp.exp(steps), dims[dim] // parts).reshape((-1,) + (1,) * (len(dims) - dim - 1))

    level = one(*pieces[0])
    for cut in pieces[1:]:
        level = level * one(*cut)
    return level


def assign_block(stream_key, own, number, rows, amount, top, bound, lean):
    ranking = jax.random.permutation(stream_key, amount)
    heavy_load, ordinary = portions_of(amount, rows * top, bound, lean, True), portions_of(amount, rows * top, bound, lean, False)
    places = jnp.arange(amount)

    def named(tallies, offset_by):
        used = int((tallies > 0).sum())
        fixed = max(1, used // 4)
        shifted = fixed + (places - fixed + offset_by * (used - fixed)) % max(1, amount - fixed)
        return jnp.zeros((amount,), jnp.int32).at[ranking[jnp.where(places < fixed, places, shifted)]].set(jnp.asarray(tallies, jnp.int32))

    tallies = jnp.where(number % 4 == 0, named(heavy_load, number // 4), named(ordinary, number - number // 4 - 1))
    mixed = jax.random.permutation(jax.random.fold_in(own, 3), amount)
    donor, taker = mixed[0:amount // 2 * 2:2], mixed[1:amount // 2 * 2:2]
    slack = jnp.minimum(tallies[donor] - 1, bound - tallies[taker]) // 2
    slack = jnp.where((donor == ranking[0]) | (taker == ranking[0]) | (tallies[taker] == 0), 0, jnp.maximum(slack, 0))
    shifted = jax.random.randint(jax.random.fold_in(own, 4), (amount // 2,), 0, 1 << 20) % (slack + 1)
    tallies = tallies.at[donor].add(-shifted).at[taker].add(shifted)
    items = jnp.searchsorted(jnp.cumsum(tallies), jnp.arange(rows * top), side="right").astype(jnp.int32)
    listing = items.reshape(top, rows).T
    listing = listing[jax.random.permutation(jax.random.fold_in(own, 1), rows)]
    offset_by = jax.random.randint(jax.random.fold_in(own, 2), (rows, 1), 0, top)
    return jnp.take_along_axis(listing, (jnp.arange(top)[None, :] + offset_by) % top, axis=1)


def portions_of(number_of, total, limit, lean, full):
    portions = [(1 << 20) // math.isqrt(standing ** lean) + 1 for standing in range(1, number_of + 1)]
    largest = limit if full else min(limit, max(-(-total // number_of), total * portions[0] // sum(portions)))
    least = 1 if total - largest >= number_of - 1 else 0
    holding, spare = [largest] + [least] * (number_of - 1), total - largest - least * (number_of - 1)
    while spare > 0:
        candidates = [i for i in range(1, number_of) if holding[i] < largest] or [i for i in range(1, number_of) if holding[i] < limit]
        pool, budget = sum([portions[i] for i in candidates]), spare
        for i in candidates:
            extra = min(limit - holding[i], max(1, budget * portions[i] // pool), spare)
            holding[i] = holding[i] + extra
            spare = spare - extra
    return np.array(holding)


def normal_values(key, extent, width, reach, shards=(), held_as=jnp.bfloat16):
    entries = width * jax.random.normal(key, extent, jnp.float32)
    if shards:
        entries = entries * level_of(key, extent, shards, -0.22, 0.18)
    return jnp.clip(entries, -reach, reach).astype(held_as)


def setup_inputs(seed: int = 0, part: int = 0) -> dict:
    seeds = jax.random.split(jax.random.key(seed), 7)
    own_keys = jax.random.split(jax.random.fold_in(seeds[6], part), 7)
    hidden_rows = normal_values(own_keys[0], (ROWS, D), 1.0, 6.0, ((0, 8), (1, 2)))
    base_out = normal_values(own_keys[1], (ROWS, OUT), 1.0, 6.0, ((0, 8), (1, 2)))
    row_adapter_keys = jax.random.split(jax.random.fold_in(own_keys[2], 1), ROWS // ROWS_DEV)
    row_adapter_turns = jax.random.permutation(jax.random.fold_in(own_keys[2], 3), ROWS // ROWS_DEV)
    row_adapter = jax.vmap(lambda own, number: assign_block(jax.random.fold_in(own_keys[2], 2), own, number, ROWS_DEV, ADAPTERS, 1, C, 2))(row_adapter_keys, row_adapter_turns).reshape((ROWS, 1))
    adapter_slot = jax.random.permutation(seeds[3], ADAPTERS).astype(jnp.int32)
    shrink_pool = normal_values(seeds[4], (ADAPTERS, D, R), D ** -0.5, 0.0625, ((0, 8), (1, 2)))
    expand_pool = normal_values(seeds[5], (ADAPTERS, R, OUT), R ** -0.5, 0.75, ((0, 8), (2, 2)))
    return dict(hidden_rows=hidden_rows, base_out=base_out, row_adapter=row_adapter, adapter_slot=adapter_slot, shrink_pool=shrink_pool, expand_pool=expand_pool)


def reference(hidden_rows, base_out, row_adapter, adapter_slot, shrink_pool, expand_pool):
    slot_ids = adapter_slot[row_adapter[:, 0]].astype(jnp.int32)
    block_rows = 32
    count_blocks = hidden_rows.shape[0] // block_rows

    def one_block(index):
        start = index * block_rows
        rows_blk = lax.dynamic_slice_in_dim(hidden_rows, start, block_rows, 0).astype(jnp.float32)
        slot_blk = lax.dynamic_slice_in_dim(slot_ids, start, block_rows, 0)
        shrink_blk = shrink_pool[slot_blk].astype(jnp.float32)
        expand_blk = expand_pool[slot_blk].astype(jnp.float32)
        latent = jnp.einsum("bd,bdr->br", rows_blk, shrink_blk).astype(jnp.bfloat16)
        update = (2.0 * jnp.einsum("br,bro->bo", latent.astype(jnp.float32), expand_blk)).astype(jnp.bfloat16)
        base_blk = lax.dynamic_slice_in_dim(base_out, start, block_rows, 0)
        return (base_blk.astype(jnp.float32) + update.astype(jnp.float32)).astype(jnp.bfloat16)

    result = lax.map(one_block, jnp.arange(count_blocks, dtype=jnp.int32))
    return result.reshape(hidden_rows.shape[0], base_out.shape[1])
```

```python
import functools
import jax
import jax.numpy as jnp
from jax import lax
from jax.experimental import pallas as pl
from jax.experimental.pallas import tpu as pltpu
from jax.sharding import PartitionSpec as P

MESH = pl.DeviceIdType.MESH
X = 2
CHUNKS = 4


def moved_rows(hidden_rows, base_out, row_adapter, adapter_slot, shrink_pool, expand_pool):
    n_pool = lax.axis_size("pool")
    rows_dev = hidden_rows.shape[0]
    capacity = 2 * max(1, rows_dev // n_pool)
    total_slots = n_pool * capacity
    adapter_ids = row_adapter[:, 0]
    count_adapters = adapter_slot.shape[0]
    matches = adapter_ids[:, None] == jnp.arange(count_adapters, dtype=jnp.int32)[None, :]
    owner_dev = jnp.sum(jnp.where(matches, adapter_slot[None, :], 0), axis=1)
    order_idx = jnp.arange(rows_dev, dtype=jnp.int32)
    earlier = (adapter_ids[:, None] == adapter_ids[None, :]) & (
        order_idx[None, :] < order_idx[:, None]
    )
    rank_in = jnp.sum(earlier.astype(jnp.int32), axis=1)
    target = owner_dev * capacity + rank_in
    onehot = (target[:, None] == jnp.arange(total_slots, dtype=jnp.int32)[None, :]).astype(
        jnp.bfloat16
    )
    packed = lax.dot_general(
        onehot, hidden_rows, (((0,), (0,)), ((), ())), preferred_element_type=jnp.float32
    )
    packed = packed.astype(jnp.bfloat16).reshape(n_pool, capacity, hidden_rows.shape[1])
    shrink_local = shrink_pool[0]
    expand_local = expand_pool[0]
    partial_latent = jnp.einsum(
        "skd,dr->skr",
        lax.all_to_all(packed, "pool", split_axis=0, concat_axis=0, tiled=True),
        shrink_local,
        preferred_element_type=jnp.float32,
    )
    latent = lax.psum(partial_latent, "tp").astype(jnp.bfloat16)
    update = (
        2.0 * jnp.einsum("skr,ro->sko", latent, expand_local, preferred_element_type=jnp.float32)
    ).astype(jnp.bfloat16)
    returned = lax.all_to_all(update, "pool", split_axis=0, concat_axis=0, tiled=True)
    flat_rows = returned.reshape(total_slots, returned.shape[2])
    unpacked = jnp.dot(onehot, flat_rows, preferred_element_type=jnp.float32)
    return (base_out.astype(jnp.float32) + unpacked).astype(jnp.bfloat16)


def kernel(n_z, hidden, ids, adapter_slot, shrink, expand, out,
           slots, s_all, h_all, id_all, e_all, part, red, lat, upd,
           loc_sem, sx_sem, s_send, s_recv, h_sem, id_sem, ex_sem, e_send, e_recv,
           rs_sem, ag_sem, u_sem):
    g = lax.axis_index("groups")
    p = lax.axis_index("pool")
    t = lax.axis_index("tp")
    z = p // X
    x = p - z * X
    rows = hidden.shape[0]
    rank = expand.shape[0]
    quarter = h_all.shape[1]
    pair = X * rank
    width = quarter // CHUNKS
    f32, bf16 = jnp.float32, jnp.bfloat16

    def flip(fg, fx, ft=0):
        return (1 - g if fg else g), (1 - x if fx else x), (1 - t if ft else t)

    def device(coords):
        return (coords[0], z * X + coords[1], coords[2])

    def up_down(up):
        return (g, p + X, t) if up else (g, p - X, t)

    q = 2 * g + x
    q_x = 2 * g + 1 - x
    planes = [(0, 1), (1, 0), (1, 1)]
    layer = [(a, b, c) for a in (0, 1) for b in (0, 1) for c in (0, 1) if a or b or c]
    pending = []

    def cols(index, size):
        return pl.ds(pl.multiple_of(index * size, size), size)

    s_copy = pltpu.make_async_copy(
        shrink.at[:, cols(q, quarter)], s_all.at[cols(p, rank)], loc_sem.at[0])
    s_copy.start()
    h_copy = pltpu.make_async_copy(
        hidden.at[:, cols(q, quarter)], h_all.at[cols(q, rows)], loc_sem.at[1])
    h_copy.start()
    e_copies = []
    for c in range(CHUNKS):
        e_copies.append(pltpu.make_async_copy(
            expand.at[:, pl.ds(pl.multiple_of(q * quarter + c * width, width), width)],
            e_all.at[c, cols(p, rank)], loc_sem.at[2 + c]))
        e_copies[-1].start()

    barrier = pltpu.get_barrier_semaphore()
    for f in layer:
        pl.semaphore_signal(barrier, inc=1, device_id=device(flip(*f)), device_id_type=MESH)

    @pl.when(z > 0)
    def _():
        pl.semaphore_signal(barrier, inc=1, device_id=up_down(False), device_id_type=MESH)

    @pl.when(z < n_z - 1)
    def _():
        pl.semaphore_signal(barrier, inc=1, device_id=up_down(True), device_id_type=MESH)

    slot = jnp.zeros(ids.shape, jnp.int32)
    for a in range(n_z * X):
        slot = jnp.where(ids[...] == a, adapter_slot[a], slot)
    slots[...] = jnp.broadcast_to(slot, slots.shape)
    id_all[q] = slots[...]

    pl.semaphore_wait(barrier, len(layer) + (z > 0).astype(jnp.int32)
                      + (z < n_z - 1).astype(jnp.int32))

    def remote(src, dst, send, recv, target):
        return pltpu.make_async_remote_copy(src_ref=src, dst_ref=dst, send_sem=send, recv_sem=recv,
                                            device_id=target, device_id_type=MESH)

    def s_hop(origin, stream, up):
        which = x if stream == 0 else 1 - x
        at = s_all.at[cols(origin * X + which, rank)]
        return remote(at, at, s_send.at[origin, stream, int(up)], s_recv.at[origin, stream],
                      up_down(up))

    def e_hop(origin, c, up):
        at = e_all.at[c, cols(origin, pair)]
        return remote(at, at, e_send.at[origin, c, int(up)], e_recv.at[origin, c], up_down(up))

    def send_own(hop):
        for up in (True, False):
            cond = z < n_z - 1 if up else z > 0

            @pl.when(cond)
            def _(up=up):
                hop(z, up).start()
            pending.append((cond, functools.partial(hop, z, up)))

    def pass_on(hop, step):
        for up in (True, False):
            origin = z - step if up else z + step
            here = (z >= step) if up else (z + step < n_z)
            onward = here & ((z < n_z - 1) if up else (z > 0))

            @pl.when(here)
            def _(origin=origin, up=up):
                hop(origin, up).wait_recv()

            @pl.when(onward)
            def _(origin=origin, up=up):
                hop(origin, up).start()
            pending.append((onward, functools.partial(hop, origin, up)))

    side = device(flip(0, 1))
    sx_copy = remote(shrink.at[:, cols(q_x, quarter)], s_all.at[cols(p, rank)],
                     sx_sem.at[0], sx_sem.at[1], side)
    sx_copy.start()
    s_copy.wait()
    send_own(lambda origin, up: s_hop(origin, 0, up))

    id_copies, h_copies = [], []
    for i, (fg, fx) in enumerate(planes):
        to = flip(fg, fx)
        there = 2 * to[0] + to[1]
        id_copies.append(remote(slots, id_all.at[q], id_sem.at[0, i], id_sem.at[1, i], device(to)))
        h_copies.append(remote(hidden.at[:, cols(there, quarter)], h_all.at[cols(q, rows)],
                               h_sem.at[0, i], h_sem.at[1, i], device(to)))
    for copy in id_copies + h_copies:
        copy.start()
    ex_copies = []
    for c in range(CHUNKS):
        ex_copies.append(remote(
            expand.at[:, pl.ds(pl.multiple_of(q_x * quarter + c * width, width), width)],
            e_all.at[c, cols(p, rank)], ex_sem.at[0, c], ex_sem.at[1, c], side))
        ex_copies[-1].start()

    sx_copy.wait_recv()
    send_own(lambda origin, up: s_hop(origin, 1, up))
    for step in range(1, n_z):
        for stream in (0, 1):
            pass_on(lambda origin, up, stream=stream: s_hop(origin, stream, up), step)

    for c in range(CHUNKS):
        e_copies[c].wait()
        ex_copies[c].wait_recv()
        send_own(lambda origin, up, c=c: e_hop(origin, c, up))

    h_copy.wait()
    for copy in id_copies + h_copies:
        copy.wait_recv()
    slot = jnp.concatenate([id_all[k][0:1, :] for k in range(2 * X)], axis=1)
    total = jnp.zeros((rank, slot.shape[1]), f32)
    for k in range(n_z):
        block = lax.dot_general(s_all[k * pair:(k + 1) * pair, :], h_all[...],
                                (((1,), (1,)), ((), ())), preferred_element_type=f32)
        for m in range(X):
            total += jnp.where(slot == k * X + m, block[m * rank:(m + 1) * rank], 0.0)
    part[...] = total

    n_layer = len(layer) + 1
    share = rank // n_layer
    mine = 2 * q + t
    rs_copies = []
    for i, f in enumerate(layer):
        to = flip(*f)
        there = 2 * (2 * to[0] + to[1]) + to[2]
        rs_copies.append(remote(part.at[cols(there, share)], red.at[i],
                                rs_sem.at[0, i], rs_sem.at[1, i], device(to)))
        rs_copies[-1].start()
    summed = part[cols(mine, share), :]
    for i, copy in enumerate(rs_copies):
        copy.wait_recv()
        summed += red[i]
    lat[cols(mine, share), :] = summed
    ag_copies = []
    for i, f in enumerate(layer):
        at = lat.at[cols(mine, share)]
        ag_copies.append(remote(at, at, ag_sem.at[0, i], ag_sem.at[1, i], device(flip(*f))))
        ag_copies[-1].start()
    for copy in ag_copies:
        copy.wait_recv()

    latent = lat[...].astype(bf16).astype(f32)
    placed = jnp.concatenate([jnp.where(slot == a, latent, 0.0).astype(bf16)
                              for a in range(n_z * X)], axis=0)
    n_rows = slot.shape[1]
    unit = (lax.broadcasted_iota(jnp.int32, (n_rows, n_rows), 0)
            == lax.broadcasted_iota(jnp.int32, (n_rows, n_rows), 1)).astype(bf16)
    placed = lax.dot_general(unit, placed, (((1,), (1,)), ((), ())),
                             preferred_element_type=f32).astype(bf16)

    u_copies = []
    for c in range(CHUNKS):
        for step in range(1, n_z):
            pass_on(lambda origin, up, c=c: e_hop(origin, c, up), step)
        upd[c] = (2.0 * jnp.dot(placed, e_all[c], preferred_element_type=f32)).astype(bf16)
        here = pl.ds(pl.multiple_of(q * quarter + c * width, width), width)
        for i, (fg, fx) in enumerate(planes):
            to = flip(fg, fx)
            there = 2 * to[0] + to[1]
            u_copies.append(remote(upd.at[c, cols(there, rows)], out.at[:, here],
                                   u_sem.at[0, c, i], u_sem.at[1, c, i], device(to)))
            u_copies[-1].start()
        out[:, here] = upd[c, cols(q, rows), :]

    for copy in u_copies:
        copy.wait_recv()
    for copy in [sx_copy] + id_copies + h_copies + ex_copies + rs_copies + ag_copies + u_copies:
        copy.wait_send()
    for cond, make in pending:
        @pl.when(cond)
        def _(make=make):
            make().wait_send()


def moved_adapters(hidden_rows, base_out, row_adapter, adapter_slot, shrink_pool, expand_pool):
    n_pool = lax.axis_size("pool")
    n_z = n_pool // X
    rows, features = hidden_rows.shape
    rank, outs = expand_pool.shape[1:]
    quarter = features // (2 * X)
    n_rows = 2 * X * rows
    bf16, f32 = jnp.bfloat16, jnp.float32
    dma = pltpu.SemaphoreType.DMA
    any_spec = pl.BlockSpec(memory_space=pl.ANY)
    vmem_spec = pl.BlockSpec(memory_space=pltpu.VMEM)
    update = pl.pallas_call(
        functools.partial(kernel, n_z),
        out_shape=jax.ShapeDtypeStruct((rows, outs), bf16),
        in_specs=[any_spec, vmem_spec, pl.BlockSpec(memory_space=pltpu.SMEM), any_spec, any_spec],
        out_specs=vmem_spec,
        scratch_shapes=[
            pltpu.VMEM((8, rows), jnp.int32),
            pltpu.VMEM((n_pool * rank, quarter), bf16),
            pltpu.VMEM((n_rows, quarter), bf16),
            pltpu.VMEM((2 * X, 8, rows), jnp.int32),
            pltpu.VMEM((CHUNKS, n_pool * rank, quarter // CHUNKS), bf16),
            pltpu.VMEM((rank, n_rows), f32),
            pltpu.VMEM((7, rank // 8, n_rows), f32),
            pltpu.VMEM((rank, n_rows), f32),
            pltpu.VMEM((CHUNKS, n_rows, quarter // CHUNKS), bf16),
            dma((2 + CHUNKS,)),
            dma((2,)),
            dma((n_z, 2, 2)),
            dma((n_z, 2)),
            dma((2, 3)),
            dma((2, 3)),
            dma((2, CHUNKS)),
            dma((n_z, CHUNKS, 2)),
            dma((n_z, CHUNKS)),
            dma((2, 7)),
            dma((2, 7)),
            dma((2, CHUNKS, 3)),
        ],
        compiler_params=pltpu.CompilerParams(
            collective_id=0, has_side_effects=True, vmem_limit_bytes=40 * 1024 * 1024),
        cost_estimate=pl.CostEstimate(
            flops=4 * rows * features * n_pool * rank, bytes_accessed=6 * 1024 * 1024,
            transcendentals=0),
    )(hidden_rows, row_adapter.reshape(1, rows), adapter_slot, shrink_pool[0].T, expand_pool[0])
    return (base_out.astype(f32) + update.astype(f32)).astype(bf16)


def solution(mesh):
    placed = (
        P(("groups", "pool"), "tp"),
        P(("groups", "pool"), "tp"),
        P(("groups", "pool"), None),
        P(),
        P("pool", "tp", None),
        P("pool", None, "tp"),
    )
    few = mesh.shape["pool"] <= 16 and mesh.shape["groups"] == 2 and mesh.shape["tp"] == 2
    local = moved_adapters if few else moved_rows
    return jax.shard_map(
        local, mesh=mesh, in_specs=placed, out_specs=P(("groups", "pool"), "tp"), check_vma=False
    )
```

```python
import functools
import jax
import jax.numpy as jnp
from jax import lax
from jax.experimental import pallas as pl
from jax.experimental.pallas import tpu as pltpu
from jax.sharding import PartitionSpec as P

MESH = pl.DeviceIdType.MESH
X = 2
CHUNKS = 4
DEPTH = 2


def moved_rows(hidden_rows, base_out, row_adapter, adapter_slot, shrink_pool, expand_pool):
    n_pool = lax.axis_size("pool")
    rows_dev = hidden_rows.shape[0]
    capacity = 2 * max(1, rows_dev // n_pool)
    total_slots = n_pool * capacity
    adapter_ids = row_adapter[:, 0]
    count_adapters = adapter_slot.shape[0]
    matches = adapter_ids[:, None] == jnp.arange(count_adapters, dtype=jnp.int32)[None, :]
    owner_dev = jnp.sum(jnp.where(matches, adapter_slot[None, :], 0), axis=1)
    order_idx = jnp.arange(rows_dev, dtype=jnp.int32)
    earlier = (adapter_ids[:, None] == adapter_ids[None, :]) & (
        order_idx[None, :] < order_idx[:, None]
    )
    rank_in = jnp.sum(earlier.astype(jnp.int32), axis=1)
    target = owner_dev * capacity + rank_in
    onehot = (target[:, None] == jnp.arange(total_slots, dtype=jnp.int32)[None, :]).astype(
        jnp.bfloat16
    )
    packed = lax.dot_general(
        onehot, hidden_rows, (((0,), (0,)), ((), ())), preferred_element_type=jnp.float32
    )
    packed = packed.astype(jnp.bfloat16).reshape(n_pool, capacity, hidden_rows.shape[1])
    shrink_local = shrink_pool[0]
    expand_local = expand_pool[0]
    partial_latent = jnp.einsum(
        "skd,dr->skr",
        lax.all_to_all(packed, "pool", split_axis=0, concat_axis=0, tiled=True),
        shrink_local,
        preferred_element_type=jnp.float32,
    )
    latent = lax.psum(partial_latent, "tp").astype(jnp.bfloat16)
    update = (
        2.0 * jnp.einsum("skr,ro->sko", latent, expand_local, preferred_element_type=jnp.float32)
    ).astype(jnp.bfloat16)
    returned = lax.all_to_all(update, "pool", split_axis=0, concat_axis=0, tiled=True)
    flat_rows = returned.reshape(total_slots, returned.shape[2])
    unpacked = jnp.dot(onehot, flat_rows, preferred_element_type=jnp.float32)
    return (base_out.astype(jnp.float32) + unpacked).astype(jnp.bfloat16)


def kernel(n_z, hidden, ids_hbm, table_hbm, shrink, expand, out,
           ids, table, slots, s_all, h_all, id_all, e_all, part, red, lat, upd,
           loc_sem, sx_sem, s_send, s_recv, h_sem, id_sem, ex_sem, e_send, e_recv,
           rs_sem, ag_sem, u_sem):
    g = lax.axis_index("groups")
    p = lax.axis_index("pool")
    t = lax.axis_index("tp")
    z = p // X
    x = p - z * X
    rows = hidden.shape[0]
    rank = expand.shape[0]
    quarter = h_all.shape[1]
    pair = X * rank
    width = quarter // CHUNKS
    f32, bf16 = jnp.float32, jnp.bfloat16

    def flip(fg, fx, ft=0):
        return (1 - g if fg else g), (1 - x if fx else x), (1 - t if ft else t)

    def device(coords):
        return (coords[0], z * X + coords[1], coords[2])

    def up_down(up):
        return (g, p + X, t) if up else (g, p - X, t)

    q = 2 * g + x
    q_x = 2 * g + 1 - x
    planes = [(0, 1), (1, 0), (1, 1)]
    layer = [(a, b, c) for a in (0, 1) for b in (0, 1) for c in (0, 1) if a or b or c]
    pending = []
    at_end = (z == 0) | (z == n_z - 1)
    inner = jnp.logical_not(at_end)
    always = z >= 0
    outward = (z == 1, z == n_z - 2)
    across = (z == n_z - 2, z == 1)

    def cols(index, size):
        return pl.ds(pl.multiple_of(index * size, size), size)

    ids_copy = pltpu.make_async_copy(ids_hbm, ids, loc_sem.at[2 + CHUNKS])
    ids_copy.start()
    table_copy = pltpu.make_async_copy(table_hbm, table, loc_sem.at[3 + CHUNKS])
    table_copy.start()
    s_copy = pltpu.make_async_copy(
        shrink.at[:, cols(q, quarter)], s_all.at[cols(p, rank)], loc_sem.at[0])
    s_copy.start()
    h_copy = pltpu.make_async_copy(
        hidden.at[:, cols(q, quarter)], h_all.at[cols(q, rows)], loc_sem.at[1])
    h_copy.start()
    e_copies = []
    for c in range(CHUNKS):
        e_copies.append(pltpu.make_async_copy(
            expand.at[:, pl.ds(pl.multiple_of(q * quarter + c * width, width), width)],
            e_all.at[c, cols(p, rank)], loc_sem.at[2 + c]))
        e_copies[-1].start()

    barrier = pltpu.get_barrier_semaphore()
    for f in layer:
        pl.semaphore_signal(barrier, inc=1, device_id=device(flip(*f)), device_id_type=MESH)

    @pl.when(z > 0)
    def _():
        pl.semaphore_signal(barrier, inc=1, device_id=up_down(False), device_id_type=MESH)

    @pl.when(z < n_z - 1)
    def _():
        pl.semaphore_signal(barrier, inc=1, device_id=up_down(True), device_id_type=MESH)

    ids_copy.wait()
    table_copy.wait()
    slot = jnp.zeros(ids.shape, jnp.int32)
    for a in range(n_z * X):
        slot = jnp.where(ids[...] == a, table[a], slot)
    slots[...] = jnp.broadcast_to(slot, slots.shape)
    id_all[q] = slots[...]

    pl.semaphore_wait(barrier, len(layer) + (z > 0).astype(jnp.int32)
                      + (z < n_z - 1).astype(jnp.int32))

    def remote(src, dst, send, recv, target):
        return pltpu.make_async_remote_copy(src_ref=src, dst_ref=dst, send_sem=send, recv_sem=recv,
                                            device_id=target, device_id_type=MESH)

    def s_hop(origin, stream, up):
        which = x if stream == 0 else 1 - x
        at = s_all.at[cols(origin * X + which, rank)]
        return remote(at, at, s_send.at[origin, stream, int(up)], s_recv.at[origin, stream],
                      up_down(up))

    def e_hop(origin, c, up):
        at = e_all.at[c, cols(origin, pair)]
        return remote(at, at, e_send.at[origin, c, int(up)], e_recv.at[origin, c], up_down(up))

    def send_own(hop, held, only=(always, always)):
        for up in (True, False):
            cond = ((z < n_z - 1) if up else (z > 0)) & only[int(up)]

            @pl.when(cond)
            def _(up=up):
                hop(z, up).start()
            held.append((cond, functools.partial(hop, z, up)))

    def drain(held, also=always):
        for cond, make in held:
            @pl.when(cond & also)
            def _(make=make):
                make().wait_send()

    def passed(step, up):
        origin = z - step if up else z + step
        here = (z >= step) if up else (z + step < n_z)
        onward = here & ((z < n_z - 1) if up else (z > 0))
        return origin, here, onward

    def pass_on(hop, step, held, only=(always, always)):
        for up in (True, False):
            origin, _, onward = passed(step, up)
            onward = onward & only[int(up)]

            @pl.when(onward)
            def _(origin=origin, up=up):
                hop(origin, up).wait_recv()
                hop(origin, up).start()
            held.append((onward, functools.partial(hop, origin, up)))

    def take(hop, step):
        for up in (True, False):
            origin, here, onward = passed(step, up)

            @pl.when(here & jnp.logical_not(onward))
            def _(origin=origin, up=up):
                hop(origin, up).wait_recv()

    def s_stream(stream):
        return lambda origin, up: s_hop(origin, stream, up)

    def e_chunk(c):
        return lambda origin, up: e_hop(origin, c, up)

    side = device(flip(0, 1))
    sx_copy = remote(shrink.at[:, cols(q_x, quarter)], s_all.at[cols(p, rank)],
                     sx_sem.at[0], sx_sem.at[1], side)
    sx_copy.start()
    s_copy.wait()
    s_own, s_passed = [], []
    send_own(s_stream(0), s_own)

    ex_copies = []
    for c in range(CHUNKS):
        ex_copies.append(remote(
            expand.at[:, pl.ds(pl.multiple_of(q_x * quarter + c * width, width), width)],
            e_all.at[c, cols(p, rank)], ex_sem.at[0, c], ex_sem.at[1, c], side))
        ex_copies[-1].start()

    id_copies, h_copies = [], []
    for i, (fg, fx) in enumerate(planes):
        to = flip(fg, fx)
        there = 2 * to[0] + to[1]
        id_copies.append(remote(slots, id_all.at[q], id_sem.at[0, i], id_sem.at[1, i], device(to)))
        h_copies.append(remote(hidden.at[:, cols(there, quarter)], h_all.at[cols(q, rows)],
                               h_sem.at[0, i], h_sem.at[1, i], device(to)))
    for copy in id_copies + h_copies:
        copy.start()
    sx_copy.wait_recv()
    send_own(s_stream(1), s_own)
    drain(s_own, at_end)
    for c in range(CHUNKS):
        @pl.when(at_end)
        def _(c=c):
            e_copies[c].wait()
            ex_copies[c].wait_recv()
        send_own(e_chunk(c), pending, (at_end, at_end))
    for step in range(1, n_z - 1):
        for stream in (0, 1):
            pass_on(s_stream(stream), step, s_passed)
    for c in range(CHUNKS):
        @pl.when(inner)
        def _(c=c):
            e_copies[c].wait()
            ex_copies[c].wait_recv()
        send_own(e_chunk(c), pending, across)
        pass_on(e_chunk(c), 1, pending, across)

    h_copy.wait()
    for copy in id_copies + h_copies:
        copy.wait_recv()
    for step in range(1, n_z):
        for stream in (0, 1):
            take(s_stream(stream), step)
    slot = jnp.concatenate([id_all[k][0:1, :] for k in range(2 * X)], axis=1)
    total = jnp.zeros((rank, slot.shape[1]), f32)
    for k in range(n_z):
        block = lax.dot_general(s_all[k * pair:(k + 1) * pair, :], h_all[...],
                                (((1,), (1,)), ((), ())), preferred_element_type=f32)
        for m in range(X):
            total += jnp.where(slot == k * X + m, block[m * rank:(m + 1) * rank], 0.0)
    part[...] = total

    n_layer = len(layer) + 1
    share = rank // n_layer
    mine = 2 * q + t
    rs_copies = []
    for i, f in enumerate(layer):
        to = flip(*f)
        there = 2 * (2 * to[0] + to[1]) + to[2]
        rs_copies.append(remote(part.at[cols(there, share)], red.at[i],
                                rs_sem.at[0, i], rs_sem.at[1, i], device(to)))
        rs_copies[-1].start()
    drain(s_own, inner)
    drain(s_passed)
    e_out = [[] for _ in range(CHUNKS)]

    def e_outward(c):
        if c >= DEPTH:
            drain(e_out[c - DEPTH])
        send_own(e_chunk(c), e_out[c], outward)
        for step in range(1, n_z - 1):
            pass_on(e_chunk(c), step, e_out[c], outward)

    for c in range(DEPTH):
        e_outward(c)
    summed = part[cols(mine, share), :]
    for i, copy in enumerate(rs_copies):
        copy.wait_recv()
        summed += red[i]
    lat[cols(mine, share), :] = summed
    ag_copies = []
    for i, f in enumerate(layer):
        at = lat.at[cols(mine, share)]
        ag_copies.append(remote(at, at, ag_sem.at[0, i], ag_sem.at[1, i], device(flip(*f))))
        ag_copies[-1].start()
    for c in range(DEPTH, CHUNKS):
        e_outward(c)
    for held in e_out[-DEPTH:]:
        pending.extend(held)
    for copy in ag_copies:
        copy.wait_recv()

    latent = lat[...].astype(bf16).astype(f32)
    placed = jnp.concatenate([jnp.where(slot == a, latent, 0.0).astype(bf16)
                              for a in range(n_z * X)], axis=0)
    n_rows = slot.shape[1]
    unit = (lax.broadcasted_iota(jnp.int32, (n_rows, n_rows), 0)
            == lax.broadcasted_iota(jnp.int32, (n_rows, n_rows), 1)).astype(bf16)
    placed = lax.dot_general(unit, placed, (((1,), (1,)), ((), ())),
                             preferred_element_type=f32).astype(bf16)

    u_copies = []
    for c in range(CHUNKS):
        for step in range(1, n_z):
            take(e_chunk(c), step)
        upd[c] = (2.0 * jnp.dot(placed, e_all[c], preferred_element_type=f32)).astype(bf16)
        here = pl.ds(pl.multiple_of(q * quarter + c * width, width), width)
        for i, (fg, fx) in enumerate(planes):
            to = flip(fg, fx)
            there = 2 * to[0] + to[1]
            u_copies.append(remote(upd.at[c, cols(there, rows)], out.at[:, here],
                                   u_sem.at[0, c, i], u_sem.at[1, c, i], device(to)))
            u_copies[-1].start()
        out[:, here] = upd[c, cols(q, rows), :]

    for copy in u_copies:
        copy.wait_recv()
    for copy in [sx_copy] + id_copies + h_copies + ex_copies + rs_copies + ag_copies + u_copies:
        copy.wait_send()
    drain(pending)


def moved_adapters(hidden_rows, base_out, row_adapter, adapter_slot, shrink_pool, expand_pool):
    n_pool = lax.axis_size("pool")
    n_z = n_pool // X
    rows, features = hidden_rows.shape
    rank, outs = expand_pool.shape[1:]
    quarter = features // (2 * X)
    n_rows = 2 * X * rows
    bf16, f32 = jnp.bfloat16, jnp.float32
    dma = pltpu.SemaphoreType.DMA
    hbm_spec = pl.BlockSpec(memory_space=pltpu.HBM)
    vmem_spec = pl.BlockSpec(memory_space=pltpu.VMEM)
    update = pl.pallas_call(
        functools.partial(kernel, n_z),
        out_shape=jax.ShapeDtypeStruct((rows, outs), bf16),
        in_specs=[hbm_spec] * 5,
        out_specs=vmem_spec,
        scratch_shapes=[
            pltpu.VMEM((1, rows), jnp.int32),
            pltpu.SMEM(adapter_slot.shape, jnp.int32),
            pltpu.VMEM((8, rows), jnp.int32),
            pltpu.VMEM((n_pool * rank, quarter), bf16),
            pltpu.VMEM((n_rows, quarter), bf16),
            pltpu.VMEM((2 * X, 8, rows), jnp.int32),
            pltpu.VMEM((CHUNKS, n_pool * rank, quarter // CHUNKS), bf16),
            pltpu.VMEM((rank, n_rows), f32),
            pltpu.VMEM((7, rank // 8, n_rows), f32),
            pltpu.VMEM((rank, n_rows), f32),
            pltpu.VMEM((CHUNKS, n_rows, quarter // CHUNKS), bf16),
            dma((4 + CHUNKS,)),
            dma((2,)),
            dma((n_z, 2, 2)),
            dma((n_z, 2)),
            dma((2, 3)),
            dma((2, 3)),
            dma((2, CHUNKS)),
            dma((n_z, CHUNKS, 2)),
            dma((n_z, CHUNKS)),
            dma((2, 7)),
            dma((2, 7)),
            dma((2, CHUNKS, 3)),
        ],
        compiler_params=pltpu.CompilerParams(
            collective_id=0, has_side_effects=True, vmem_limit_bytes=60 * 1024 * 1024),
        cost_estimate=pl.CostEstimate(
            flops=4 * rows * features * n_pool * rank, bytes_accessed=6 * 1024 * 1024,
            transcendentals=0),
    )(hidden_rows, row_adapter.reshape(1, rows), adapter_slot, shrink_pool[0].T, expand_pool[0])
    return (base_out.astype(f32) + update.astype(f32)).astype(bf16)


def solution(mesh):
    placed = (
        P(("groups", "pool"), "tp"),
        P(("groups", "pool"), "tp"),
        P(("groups", "pool"), None),
        P(),
        P("pool", "tp", None),
        P("pool", None, "tp"),
    )
    few = mesh.shape["pool"] == 4 * X and mesh.shape["groups"] == 2 and mesh.shape["tp"] == 2
    local = moved_adapters if few else moved_rows
    return jax.shard_map(
        local, mesh=mesh, in_specs=placed, out_specs=P(("groups", "pool"), "tp"), check_vma=False
    )
```

```python
import functools
import jax
import jax.numpy as jnp
from jax import lax
from jax.experimental import pallas as pl
from jax.experimental.pallas import tpu as pltpu
from jax.sharding import PartitionSpec as P

MESH = pl.DeviceIdType.MESH
X = 2
CHUNKS = 4
DEPTH = 2


def moved_rows(hidden_rows, base_out, row_adapter, adapter_slot, shrink_pool, expand_pool):
    n_pool = lax.axis_size("pool")
    rows_dev = hidden_rows.shape[0]
    capacity = 2 * max(1, rows_dev // n_pool)
    total_slots = n_pool * capacity
    adapter_ids = row_adapter[:, 0]
    count_adapters = adapter_slot.shape[0]
    matches = adapter_ids[:, None] == jnp.arange(count_adapters, dtype=jnp.int32)[None, :]
    owner_dev = jnp.sum(jnp.where(matches, adapter_slot[None, :], 0), axis=1)
    order_idx = jnp.arange(rows_dev, dtype=jnp.int32)
    earlier = (adapter_ids[:, None] == adapter_ids[None, :]) & (
        order_idx[None, :] < order_idx[:, None]
    )
    rank_in = jnp.sum(earlier.astype(jnp.int32), axis=1)
    target = owner_dev * capacity + rank_in
    onehot = (target[:, None] == jnp.arange(total_slots, dtype=jnp.int32)[None, :]).astype(
        jnp.bfloat16
    )
    packed = lax.dot_general(
        onehot, hidden_rows, (((0,), (0,)), ((), ())), preferred_element_type=jnp.float32
    )
    packed = packed.astype(jnp.bfloat16).reshape(n_pool, capacity, hidden_rows.shape[1])
    shrink_local = shrink_pool[0]
    expand_local = expand_pool[0]
    partial_latent = jnp.einsum(
        "skd,dr->skr",
        lax.all_to_all(packed, "pool", split_axis=0, concat_axis=0, tiled=True),
        shrink_local,
        preferred_element_type=jnp.float32,
    )
    latent = lax.psum(partial_latent, "tp").astype(jnp.bfloat16)
    update = (
        2.0 * jnp.einsum("skr,ro->sko", latent, expand_local, preferred_element_type=jnp.float32)
    ).astype(jnp.bfloat16)
    returned = lax.all_to_all(update, "pool", split_axis=0, concat_axis=0, tiled=True)
    flat_rows = returned.reshape(total_slots, returned.shape[2])
    unpacked = jnp.dot(onehot, flat_rows, preferred_element_type=jnp.float32)
    return (base_out.astype(jnp.float32) + unpacked).astype(jnp.bfloat16)


def kernel(n_z, hidden, ids_hbm, table_hbm, shrink, expand, out,
           ids, table, slots, s_all, h_all, id_all, e_all, part, red, lat, upd,
           loc_sem, sx_sem, s_send, s_recv, h_sem, id_sem, ex_sem, e_send, e_recv,
           rs_sem, ag_sem, u_sem, own_sem):
    g = lax.axis_index("groups")
    p = lax.axis_index("pool")
    t = lax.axis_index("tp")
    z = p // X
    x = p - z * X
    rows = hidden.shape[0]
    rank = expand.shape[0]
    quarter = h_all.shape[1]
    pair = X * rank
    width = quarter // CHUNKS
    f32, bf16 = jnp.float32, jnp.bfloat16

    def flip(fg, fx, ft=0):
        return (1 - g if fg else g), (1 - x if fx else x), (1 - t if ft else t)

    def device(coords):
        return (coords[0], z * X + coords[1], coords[2])

    def up_down(up):
        return (g, p + X, t) if up else (g, p - X, t)

    q = 2 * g + x
    q_x = 2 * g + 1 - x
    planes = [(0, 1), (1, 0), (1, 1)]
    layer = [(a, b, c) for a in (0, 1) for b in (0, 1) for c in (0, 1) if a or b or c]
    pending = []
    at_end = (z == 0) | (z == n_z - 1)
    inner = jnp.logical_not(at_end)
    always = z >= 0
    outward = (z == 1, z == n_z - 2)
    across = (z == n_z - 2, z == 1)

    def cols(index, size):
        return pl.ds(pl.multiple_of(index * size, size), size)

    ids_copy = pltpu.make_async_copy(ids_hbm, ids, loc_sem.at[2 + CHUNKS])
    ids_copy.start()
    table_copy = pltpu.make_async_copy(table_hbm, table, loc_sem.at[3 + CHUNKS])
    table_copy.start()
    s_copy = pltpu.make_async_copy(
        shrink.at[:, cols(q, quarter)], s_all.at[cols(p, rank)], loc_sem.at[0])
    s_copy.start()
    h_copy = pltpu.make_async_copy(
        hidden.at[:, cols(q, quarter)], h_all.at[cols(q, rows)], loc_sem.at[1])
    h_copy.start()
    e_copies = []
    for c in range(CHUNKS):
        e_copies.append(pltpu.make_async_copy(
            expand.at[:, pl.ds(pl.multiple_of(q * quarter + c * width, width), width)],
            e_all.at[c, cols(p, rank)], loc_sem.at[2 + c]))
        e_copies[-1].start()

    barrier = pltpu.get_barrier_semaphore()
    for f in layer:
        pl.semaphore_signal(barrier, inc=1, device_id=device(flip(*f)), device_id_type=MESH)

    @pl.when(z > 0)
    def _():
        pl.semaphore_signal(barrier, inc=1, device_id=up_down(False), device_id_type=MESH)

    @pl.when(z < n_z - 1)
    def _():
        pl.semaphore_signal(barrier, inc=1, device_id=up_down(True), device_id_type=MESH)

    ids_copy.wait()
    table_copy.wait()
    slot = jnp.zeros(ids.shape, jnp.int32)
    for a in range(n_z * X):
        slot = jnp.where(ids[...] == a, table[a], slot)
    slots[...] = jnp.broadcast_to(slot, slots.shape)
    id_all[q] = slots[...]

    pl.semaphore_wait(barrier, len(layer) + (z > 0).astype(jnp.int32)
                      + (z < n_z - 1).astype(jnp.int32))

    def remote(src, dst, send, recv, target):
        return pltpu.make_async_remote_copy(src_ref=src, dst_ref=dst, send_sem=send, recv_sem=recv,
                                            device_id=target, device_id_type=MESH)

    def s_hop(origin, stream, up):
        which = x if stream == 0 else 1 - x
        at = s_all.at[cols(origin * X + which, rank)]
        return remote(at, at, s_send.at[origin, stream, int(up)], s_recv.at[origin, stream],
                      up_down(up))

    def e_hop(origin, c, up):
        at = e_all.at[c, cols(origin, pair)]
        return remote(at, at, e_send.at[origin, c, int(up)], e_recv.at[origin, c], up_down(up))

    def send_own(hop, held, only=(always, always)):
        for up in (True, False):
            cond = ((z < n_z - 1) if up else (z > 0)) & only[int(up)]

            @pl.when(cond)
            def _(up=up):
                hop(z, up).start()
            held.append((cond, functools.partial(hop, z, up)))

    def drain(held, also=always):
        for cond, make in held:
            @pl.when(cond & also)
            def _(make=make):
                make().wait_send()

    def passed(step, up):
        origin = z - step if up else z + step
        here = (z >= step) if up else (z + step < n_z)
        onward = here & ((z < n_z - 1) if up else (z > 0))
        return origin, here, onward

    def pass_on(hop, step, held, only=(always, always)):
        for up in (True, False):
            origin, _, onward = passed(step, up)
            onward = onward & only[int(up)]

            @pl.when(onward)
            def _(origin=origin, up=up):
                hop(origin, up).wait_recv()
                hop(origin, up).start()
            held.append((onward, functools.partial(hop, origin, up)))

    def take(hop, step):
        for up in (True, False):
            origin, here, onward = passed(step, up)

            @pl.when(here & jnp.logical_not(onward))
            def _(origin=origin, up=up):
                hop(origin, up).wait_recv()

    def s_stream(stream):
        return lambda origin, up: s_hop(origin, stream, up)

    def e_chunk(c):
        return lambda origin, up: e_hop(origin, c, up)

    side = device(flip(0, 1))
    sx_copy = remote(shrink.at[:, cols(q_x, quarter)], s_all.at[cols(p, rank)],
                     sx_sem.at[0], sx_sem.at[1], side)
    sx_copy.start()
    s_copy.wait()
    s_own, s_passed = [], []
    send_own(s_stream(0), s_own)

    ex_copies = []
    for c in range(CHUNKS):
        ex_copies.append(remote(
            expand.at[:, pl.ds(pl.multiple_of(q_x * quarter + c * width, width), width)],
            e_all.at[c, cols(p, rank)], ex_sem.at[0, c], ex_sem.at[1, c], side))
        ex_copies[-1].start()

    id_copies, h_copies = [], []
    for i, (fg, fx) in enumerate(planes):
        to = flip(fg, fx)
        there = 2 * to[0] + to[1]
        id_copies.append(remote(slots, id_all.at[q], id_sem.at[0, i], id_sem.at[1, i], device(to)))
        h_copies.append(remote(hidden.at[:, cols(there, quarter)], h_all.at[cols(q, rows)],
                               h_sem.at[0, i], h_sem.at[1, i], device(to)))
    for copy in id_copies + h_copies:
        copy.start()
    sx_copy.wait_recv()
    send_own(s_stream(1), s_own)
    drain(s_own, at_end)
    for c in range(CHUNKS):
        @pl.when(at_end)
        def _(c=c):
            e_copies[c].wait()
            ex_copies[c].wait_recv()
        send_own(e_chunk(c), pending, (at_end, at_end))
    for step in range(1, n_z - 1):
        for stream in (0, 1):
            pass_on(s_stream(stream), step, s_passed)
    for c in range(CHUNKS):
        @pl.when(inner)
        def _(c=c):
            e_copies[c].wait()
            ex_copies[c].wait_recv()
        send_own(e_chunk(c), pending, across)
        pass_on(e_chunk(c), 1, pending, across)

    h_copy.wait()
    for copy in id_copies + h_copies:
        copy.wait_recv()
    for step in range(1, n_z):
        for stream in (0, 1):
            take(s_stream(stream), step)
    slot = jnp.concatenate([id_all[k][0:1, :] for k in range(2 * X)], axis=1)
    total = jnp.zeros((rank, slot.shape[1]), f32)
    for k in range(n_z):
        block = lax.dot_general(s_all[k * pair:(k + 1) * pair, :], h_all[...],
                                (((1,), (1,)), ((), ())), preferred_element_type=f32)
        for m in range(X):
            total += jnp.where(slot == k * X + m, block[m * rank:(m + 1) * rank], 0.0)
    part[...] = total

    n_layer = len(layer) + 1
    share = rank // n_layer
    mine = 2 * q + t
    rs_copies = []
    for i, f in enumerate(layer):
        to = flip(*f)
        there = 2 * (2 * to[0] + to[1]) + to[2]
        rs_copies.append(remote(part.at[cols(there, share)], red.at[i],
                                rs_sem.at[0, i], rs_sem.at[1, i], device(to)))
        rs_copies[-1].start()
    drain(s_own, inner)
    drain(s_passed)
    e_out = [[] for _ in range(CHUNKS)]

    def e_outward(c):
        if c >= DEPTH:
            drain(e_out[c - DEPTH])
        send_own(e_chunk(c), e_out[c], outward)
        for step in range(1, n_z - 1):
            pass_on(e_chunk(c), step, e_out[c], outward)

    for c in range(DEPTH):
        e_outward(c)
    summed = part[cols(mine, share), :]
    for i, copy in enumerate(rs_copies):
        copy.wait_recv()
        summed += red[i]
    lat[cols(mine, share), :] = summed
    ag_copies = []
    for i, f in enumerate(layer):
        at = lat.at[cols(mine, share)]
        ag_copies.append(remote(at, at, ag_sem.at[0, i], ag_sem.at[1, i], device(flip(*f))))
        ag_copies[-1].start()
    for c in range(DEPTH, CHUNKS):
        e_outward(c)
    for held in e_out[-DEPTH:]:
        pending.extend(held)
    for copy in ag_copies:
        copy.wait_recv()

    latent = lat[...].astype(bf16).astype(f32)
    placed = jnp.concatenate([jnp.where(slot == a, latent, 0.0).astype(bf16)
                              for a in range(n_z * X)], axis=0)
    n_rows = slot.shape[1]
    unit = (lax.broadcasted_iota(jnp.int32, (n_rows, n_rows), 0)
            == lax.broadcasted_iota(jnp.int32, (n_rows, n_rows), 1)).astype(bf16)
    placed = lax.dot_general(unit, placed, (((1,), (1,)), ((), ())),
                             preferred_element_type=f32).astype(bf16)

    u_copies, own_copies = [], []
    for c in range(CHUNKS):
        for step in range(1, n_z):
            take(e_chunk(c), step)
        upd[c] = (2.0 * jnp.dot(placed, e_all[c], preferred_element_type=f32)).astype(bf16)
        here = pl.ds(pl.multiple_of(q * quarter + c * width, width), width)
        for i, (fg, fx) in enumerate(planes):
            to = flip(fg, fx)
            there = 2 * to[0] + to[1]
            u_copies.append(remote(upd.at[c, cols(there, rows)], out.at[:, here],
                                   u_sem.at[0, c, i], u_sem.at[1, c, i], device(to)))
            u_copies[-1].start()
        own_copies.append(pltpu.make_async_copy(upd.at[c, cols(q, rows)], out.at[:, here],
                                                own_sem.at[c]))
        own_copies[-1].start()

    for copy in u_copies:
        copy.wait_recv()
    for copy in [sx_copy] + id_copies + h_copies + ex_copies + rs_copies + ag_copies + u_copies:
        copy.wait_send()
    for copy in own_copies:
        copy.wait()
    drain(pending)


def moved_adapters(hidden_rows, base_out, row_adapter, adapter_slot, shrink_pool, expand_pool):
    n_pool = lax.axis_size("pool")
    n_z = n_pool // X
    rows, features = hidden_rows.shape
    rank, outs = expand_pool.shape[1:]
    quarter = features // (2 * X)
    n_rows = 2 * X * rows
    bf16, f32 = jnp.bfloat16, jnp.float32
    dma = pltpu.SemaphoreType.DMA
    hbm_spec = pl.BlockSpec(memory_space=pltpu.HBM)
    update = pl.pallas_call(
        functools.partial(kernel, n_z),
        out_shape=jax.ShapeDtypeStruct((rows, outs), bf16),
        in_specs=[hbm_spec] * 5,
        out_specs=hbm_spec,
        scratch_shapes=[
            pltpu.VMEM((1, rows), jnp.int32),
            pltpu.SMEM(adapter_slot.shape, jnp.int32),
            pltpu.VMEM((8, rows), jnp.int32),
            pltpu.VMEM((n_pool * rank, quarter), bf16),
            pltpu.VMEM((n_rows, quarter), bf16),
            pltpu.VMEM((2 * X, 8, rows), jnp.int32),
            pltpu.VMEM((CHUNKS, n_pool * rank, quarter // CHUNKS), bf16),
            pltpu.VMEM((rank, n_rows), f32),
            pltpu.VMEM((7, rank // 8, n_rows), f32),
            pltpu.VMEM((rank, n_rows), f32),
            pltpu.VMEM((CHUNKS, n_rows, quarter // CHUNKS), bf16),
            dma((4 + CHUNKS,)),
            dma((2,)),
            dma((n_z, 2, 2)),
            dma((n_z, 2)),
            dma((2, 3)),
            dma((2, 3)),
            dma((2, CHUNKS)),
            dma((n_z, CHUNKS, 2)),
            dma((n_z, CHUNKS)),
            dma((2, 7)),
            dma((2, 7)),
            dma((2, CHUNKS, 3)),
            dma((CHUNKS,)),
        ],
        compiler_params=pltpu.CompilerParams(
            collective_id=0, has_side_effects=True, vmem_limit_bytes=60 * 1024 * 1024),
        cost_estimate=pl.CostEstimate(
            flops=4 * rows * features * n_pool * rank, bytes_accessed=6 * 1024 * 1024,
            transcendentals=0),
    )(hidden_rows, row_adapter.reshape(1, rows), adapter_slot, shrink_pool[0].T, expand_pool[0])
    return (base_out.astype(f32) + update.astype(f32)).astype(bf16)


def solution(mesh):
    placed = (
        P(("groups", "pool"), "tp"),
        P(("groups", "pool"), "tp"),
        P(("groups", "pool"), None),
        P(),
        P("pool", "tp", None),
        P("pool", None, "tp"),
    )
    few = mesh.shape["pool"] == 4 * X and mesh.shape["groups"] == 2 and mesh.shape["tp"] == 2
    local = moved_adapters if few else moved_rows
    return jax.shard_map(
        local, mesh=mesh, in_specs=placed, out_specs=P(("groups", "pool"), "tp"), check_vma=False
    )
```
